256 devices in a mesh: ia: 4 (over y), ja: 16 (over z, core), ka: 4 (over x).
Axes of the slice: x: 4, y: 4, z: 8, core: 2. Of those that a mesh axis runs over, the one named last changes fastest.
Arguments:
- tensor: bfloat16 [64, 4096, 4096], P('ia', 'ja', 'ka'), may hold values from -6 to 6
- factor_j: bfloat16 [25, 4096], P(None, ('ja', 'ka', 'ia'))
- factor_k: bfloat16 [25, 4096], P(None, ('ka', 'ja'))
Outputs:
- y_part: float32 [25, 64, 4096], P(None, 'ia', ('ja', 'ka'))
- new_factor: float32 [25, 64], P(None, 'ia')
The draws below stay inside these ranges and needn't reach their ends.
All inputs are finite; a program needn't handle non-finite values.
Results may differ from the reference program's by a relative error of at most 0.0003.
Values may be sent and summed in bfloat16 or wider, within the bound.
No kernel may reach another device: no remote copies, remote signals or barrier semaphores. Data moves between devices by JAX's collectives and lax.ppermute only.
A program may use at most 64 MiB of HBM per device.

```python
import math
import jax
import jax.numpy as jnp
from jax import lax

RANK = 25
I = 64
J = 4096
K = 4096


def factor_rows(own, common, share, width, key):
    spread = jnp.exp(jax.random.uniform(key, (RANK, 1), jnp.float32, math.log(0.5), math.log(2.0)))
    return ((own + share * common) * spread / math.sqrt(width * (1.0 + share * share))).astype(jnp.bfloat16)


def draw_factor_j(key, part):
    key = jax.random.fold_in(key, 1)
    first, second, third = jax.random.split(key, 3)
    own = jnp.clip(jax.random.normal(first, (RANK, J), jnp.float32), -4.0, 4.0)
    common = jnp.clip(jax.random.normal(second, (1, J), jnp.float32), -4.0, 4.0)
    return factor_rows(own, common, 0.9, J, third)


def draw_factor_k(key, part):
    key = jax.random.fold_in(key, 2)
    first, second, third = jax.random.split(key, 3)
    own = jnp.clip(jax.random.normal(first, (RANK, K), jnp.float32), -4.0, 4.0)
    common = jnp.clip(jax.random.normal(second, (1, K), jnp.float32), -4.0, 4.0)
    return factor_rows(own, common, 0.9, K, third)


def shard_levels(own_key, shape, cuts, smallest, high):
    loudness = 1.0
    for position, blocks in cuts:
        heights = jax.random.uniform(jax.random.fold_in(jax.random.fold_in(own_key, 6), position), (blocks,), jnp.float32, smallest / len(cuts), high / len(cuts))
        loudness = loudness * jnp.repeat(jnp.exp(heights), shape[position] // blocks).reshape((-1,) + (1,) * (len(shape) - 1 - position))
    return loudness


def normal_values(own_key, shape, scale, most, pieces=(), held_as=jnp.bfloat16):
    drawn = scale * jax.random.normal(own_key, shape, jnp.float32)
    if pieces:
        drawn = drawn * shard_levels(own_key, shape, pieces, -0.22, 0.18)
    return jnp.clip(drawn, -most, most).astype(held_as)


def setup_inputs(seed: int = 0) -> dict:
    keys = jax.random.split(jax.random.key(seed), 4)
    tensor = normal_values(keys[0], (I, J, K), 1.0, 6.0, ((0, 4), (1, 16), (2, 4)))
    factor_j = draw_factor_j(jax.random.fold_in(keys[3], 71), 0)
    factor_k = draw_factor_k(jax.random.fold_in(keys[3], 71), 0)
    return dict(tensor=tensor, factor_j=factor_j, factor_k=factor_k)


def gram_of(factor):
    return jnp.dot(factor.astype(jnp.float32), factor.T.astype(jnp.float32), preferred_element_type=jnp.float32)

def reference(tensor, factor_j, factor_k):
    flat = tensor.reshape(I * J, K)
    y_part = lax.dot_general(factor_k.astype(jnp.float32), flat.astype(jnp.float32), (((1,), (1,)), ((), ())), preferred_element_type=jnp.float32).reshape(RANK, I, J)
    mttkrp = jnp.einsum('rij,rj->ri', y_part, factor_j.astype(jnp.float32), precision=lax.Precision.HIGHEST)
    normal_matrix = gram_of(factor_j) * gram_of(factor_k)
    lower = jnp.linalg.cholesky(normal_matrix)
    new_factor = jax.scipy.linalg.cho_solve((lower, True), mttkrp)
    return (y_part, new_factor)
```

```python
import functools

import jax
import jax.numpy as jnp
from jax import lax
from jax.experimental import pallas as pl
from jax.experimental.pallas import tpu as pltpu
from jax.sharding import PartitionSpec as P

f32, bf16 = jnp.float32, jnp.bfloat16
R = 25
VM = pl.BlockSpec(memory_space=pltpu.VMEM)
HB = pl.BlockSpec(memory_space=pltpu.HBM)
TILES, BODY, MSG = 8, 200, 208
BLOCK = 5


def lanes_of(shape):
    return lax.broadcasted_iota(jnp.int32, shape, 1)


def sublanes_of(shape):
    return lax.broadcasted_iota(jnp.int32, shape, 0)


def pad_rows(x, rows):
    return jnp.concatenate([x, jnp.zeros((rows - x.shape[0], x.shape[1]), x.dtype)], axis=0)


def pack_kernel(k_ref, out_ref, k_vmem, sem):
    copy = pltpu.make_async_copy(k_ref, k_vmem, sem)
    copy.start()
    copy.wait()
    k = pad_rows(k_vmem[...].astype(f32), 32)
    folded = jnp.concatenate([k[0:16], k[16:32]], axis=1).astype(bf16)
    out_ref[...] = jnp.broadcast_to(folded[None], out_ref.shape)


def contract_kernel(c_ref, t_ref, *refs):
    msgs, t_vmem, sems = refs[0:4], refs[4], refs[5]
    here = lax.axis_index("ka")

    def copy(s, h):
        dest = lax.rem(here + s, 4)
        block = t_ref.at[pl.ds(8 * h, 8), pl.ds(pl.multiple_of(dest * 64, 64), 64), :]
        return pltpu.make_async_copy(block, t_vmem.at[s, pl.ds(8 * h, 8)], sems.at[s, h])

    order = [(s, h) for s in (2, 1, 3, 0) for h in (0, 1)]
    for s, h in order:
        copy(s, h).start()
    blocks = [c_ref[p].astype(f32) for p in range(16)]
    low = lanes_of((16, 128)) < 64
    tops, bottoms = [], []
    for a, b in zip(blocks[0::2], blocks[1::2]):
        tops.append(jnp.where(low, a, pltpu.roll(b, 64, 1)))
        bottoms.append(jnp.where(low, pltpu.roll(a, 64, 1), b))
    c = jnp.concatenate([jnp.concatenate(tops, axis=1), jnp.concatenate(bottoms, axis=1)], axis=0).astype(bf16)
    nt = (((1,), (1,)), ((), ()))
    gram = lax.dot_general(c, c, nt, preferred_element_type=f32)
    gram = jnp.concatenate([gram[8 * q : 8 * q + 8] for q in range(4)], axis=1)
    for s, h in order:
        msg = msgs[s]
        copy(s, h).wait()
        y = lax.dot_general(c, t_vmem[s, 8 * h : 8 * h + 8].reshape(512, 1024), nt, preferred_element_type=f32)
        for t in range(4):
            u = 4 * h + t
            msg[24 * u : 24 * u + 24, :] = y[0:24, 128 * t : 128 * t + 128]
            msg[192 + u : 193 + u, :] = y[24:25, 128 * t : 128 * t + 128]
        if h == 0:
            msg[BODY:MSG, :] = gram


def factor_kernel(j0, j1, j2, j3, b_ref, gram_ref):
    b = jnp.concatenate([j[...].astype(f32) for j in (j0, j3, j2, j1)], axis=0)
    b = pad_rows(jnp.concatenate([b, jnp.zeros((64, 128 - R), f32)], axis=1), 128).T[0:32, 0:64]
    bb = b.astype(bf16)
    gram = lax.dot_general(bb, bb, (((1,), (1,)), ((), ())), preferred_element_type=f32)
    gram_ref[...] = jnp.concatenate([gram, jnp.zeros((32, 96), f32)], axis=1)
    b_ref[...] = pltpu.roll(jnp.concatenate([b, b], axis=1), lax.axis_index("ia") * 16, 1)


def share_kernel(y0, y1, y2, y3, b_ref, gram_ref, s_ref, pay_ref, gk_ref):
    b = b_ref[...]
    gram_j = gram_ref[:, 0:32]
    gk_ref[...] = (y0[BODY:MSG, :] + y1[BODY:MSG, :]) + (y2[BODY:MSG, :] + y3[BODY:MSG, :])
    lane24, low24 = lanes_of((24, 128)), lanes_of((24, 128)) < 64
    m = jnp.zeros((24, 128), f32)
    for t in range(TILES):
        at = slice(24 * t, 24 * t + 24)
        s = (y0[at, :] + y1[at, :]) + (y2[at, :] + y3[at, :])
        s_ref[at, :] = s
        p = s * b[0:24]
        m = jnp.where(lane24 == 2 * t, jnp.sum(jnp.where(low24, p, 0.0), axis=1, keepdims=True), m)
        m = jnp.where(lane24 == 2 * t + 1, jnp.sum(jnp.where(low24, 0.0, p), axis=1, keepdims=True), m)
    at = slice(192, 200)
    s = (y0[at, :] + y1[at, :]) + (y2[at, :] + y3[at, :])
    s_ref[at, :] = s
    p = s * b[24:25]
    lane8, sub8 = lanes_of((8, 128)), sublanes_of((8, 128))
    low8 = lane8 < 64
    last = jnp.where(lane8 == 2 * sub8, jnp.sum(jnp.where(low8, p, 0.0), axis=1, keepdims=True), 0.0)
    last = last + jnp.where(lane8 == 2 * sub8 + 1, jnp.sum(jnp.where(low8, 0.0, p), axis=1, keepdims=True), 0.0)
    last = jnp.sum(last, axis=0, keepdims=True)
    m = pad_rows(jnp.concatenate([m, last], axis=0), 32)
    x = jnp.concatenate([m[:, 0:16], gram_j, jnp.zeros((32, 16), f32)], axis=1)
    pay_ref[...] = jnp.broadcast_to(jnp.concatenate([x[0:16], x[16:32]], axis=1)[None], pay_ref.shape)


def unfold_kernel(s_ref, y_ref):
    for t in range(TILES):
        s = s_ref[24 * t : 24 * t + 24, :]
        y_ref[pl.ds(2 * t, 24, stride=16), :] = s[:, 0:64]
        y_ref[pl.ds(2 * t + 1, 24, stride=16), :] = s[:, 64:128]
    s = s_ref[192:200, :]
    y_ref[pl.ds(384, 8, stride=2), :] = s[:, 0:64]
    y_ref[pl.ds(385, 8, stride=2), :] = s[:, 64:128]


def sum_kernel(x_ref, out_ref):
    out_ref[...] = jnp.sum(x_ref[...], axis=0)


def solve_kernel(x0, x1, gk_ref, out_ref):
    x = x0[...] + x1[...]
    x = jnp.concatenate([x[:, 0:64], x[:, 64:128]], axis=0)
    gk = gk_ref[...]
    gram_k = jnp.concatenate([gk[:, 32 * q : 32 * q + 32] for q in range(4)], axis=0)
    n = x[:, 16:48] * gram_k
    a = jnp.concatenate([n, x[:, 0:16], jnp.zeros((32, 80), f32)], axis=1)
    row_at = sublanes_of((32, 128))
    for first in range(0, R, BLOCK):
        cols = [jnp.broadcast_to(a[:, p : p + 1], (32, 128)) for p in range(first, min(first + BLOCK, R))]
        for q in range(len(cols)):
            p = first + q
            scale = 1.0 / cols[q][p : p + 1, :]

            def eliminate(x):
                row = jnp.broadcast_to(x[p : p + 1, :] * scale, (32, 128))
                return jnp.where(row_at == p, row, x - cols[q] * row)

            a = eliminate(a)
            cols[q + 1 :] = [eliminate(x) for x in cols[q + 1 :]]
    out_ref[...] = pad_rows(a, 128).T[32:48, 0:R]


def call(kernel, out, specs, flops=0, nbytes=0, scratch=()):
    return pl.pallas_call(
        kernel,
        out_shape=out,
        in_specs=specs,
        out_specs=jax.tree.map(lambda _: VM, out),
        scratch_shapes=scratch,
        compiler_params=pltpu.CompilerParams(vmem_limit_bytes=16 * 2**20),
        cost_estimate=pl.CostEstimate(flops=flops, bytes_accessed=nbytes, transcendentals=0),
    )


def shift(x, axis, by, n):
    return lax.ppermute(x, axis, [(i, (i + by) % n) for i in range(n)])


def per_device(tensor, factor_j, factor_k):
    sds = jax.ShapeDtypeStruct
    dma = pltpu.SemaphoreType.DMA
    factor_k = pltpu.with_memory_space_constraint(factor_k, pltpu.HBM)
    tensor = pltpu.with_memory_space_constraint(tensor, pltpu.HBM)
    j0 = factor_j.T
    j1 = shift(j0, "ia", 1, 4)
    j3 = shift(j0, "ia", 3, 4)
    packed = call(pack_kernel, sds((16, 16, 128), bf16), [HB], scratch=[pltpu.VMEM((R, 64), bf16), dma(())])(factor_k)
    c = lax.all_to_all(packed, ("z", "c"), 0, 0, tiled=True)
    c, j1, j3 = lax.optimization_barrier((c, j1, j3))
    j2 = shift(j1, "ia", 1, 4)
    msgs = call(
        contract_kernel, [sds((MSG, 128), f32)] * 4, [VM, HB], 2**28, 2**23,
        [pltpu.VMEM((4, 16, 64, 1024), bf16), dma((4, 2))],
    )(c, tensor)
    got = [shift(msgs[s], "ka", s, 4) for s in (1, 2, 3)]
    b, gram_j = call(factor_kernel, [sds((32, 128), f32)] * 2, [VM] * 4)(j0, j1, j2, j3)
    total, pay, gram_k = call(
        share_kernel, [sds((BODY, 128), f32), sds((32, 16, 128), f32), sds((8, 128), f32)], [VM] * 6
    )(msgs[0], *got, b, gram_j)
    pay = lax.all_to_all(pay, ("z", "ka"), 0, 0, tiled=True)
    x = call(sum_kernel, sds((16, 128), f32), [VM])(pay)
    other = lax.ppermute(x, "c", [(0, 1), (1, 0)])
    y = call(unfold_kernel, sds((400, 64), f32), [VM], 0, 2**21)(total)
    new_factor = call(solve_kernel, sds((16, R), f32), [VM] * 3)(x, other, gram_k)
    return y.reshape(R, 16, 64), new_factor.T


def solution(mesh):
    ia, ja, ka = (mesh.shape[a] for a in ("ia", "ja", "ka"))
    mesh = jax.sharding.Mesh(mesh.devices.reshape(ia, ja // 2, 2, ka), ("ia", "z", "c", "ka"))
    in_specs = (P("ia", ("z", "c"), "ka"), P(None, ("z", "c", "ka", "ia")), P(None, ("ka", "z", "c")))
    out_specs = (P(None, "ia", ("z", "c", "ka")), P(None, "ia"))
    return jax.shard_map(
        per_device, mesh=mesh, in_specs=in_specs, out_specs=out_specs, check_vma=False
    )
```

```python
import functools

import jax
import jax.numpy as jnp
from jax import lax
from jax.experimental import pallas as pl
from jax.experimental.pallas import tpu as pltpu
from jax.sharding import PartitionSpec as P

f32, bf16 = jnp.float32, jnp.bfloat16
R = 25
VM = pl.BlockSpec(memory_space=pltpu.VMEM)
HB = pl.BlockSpec(memory_space=pltpu.HBM)
TILES, BODY, MSG = 8, 200, 208
DIAGONALS = 13
BLOCK = 13


def lanes_of(shape):
    return lax.broadcasted_iota(jnp.int32, shape, 1)


def sublanes_of(shape):
    return lax.broadcasted_iota(jnp.int32, shape, 0)


def pad_rows(x, rows):
    return jnp.concatenate([x, jnp.zeros((rows - x.shape[0], x.shape[1]), x.dtype)], axis=0)


def fold(g):
    return jnp.concatenate([g[8 * q : 8 * q + 8] for q in range(4)], axis=1)


def unfold(g):
    return jnp.concatenate([g[:, 32 * q : 32 * q + 32] for q in range(4)], axis=0)


def transposed(x):
    rows = -(-x.shape[1] // 8) * 8
    x = jnp.concatenate([x, jnp.zeros((x.shape[0], 128 - x.shape[1]), x.dtype)], axis=1)
    return pad_rows(x, 128).T[0:rows, 0 : x.shape[0]]


def pack_kernel(k_ref, out_ref, k_vmem, sem):
    copy = pltpu.make_async_copy(k_ref, k_vmem, sem)
    copy.start()
    copy.wait()
    k = pad_rows(k_vmem[...].astype(f32), 32)
    folded = jnp.concatenate([k[0:16], k[16:32]], axis=1).astype(bf16)
    out_ref[...] = jnp.broadcast_to(folded[None], out_ref.shape)


def factor_kernel(j0, j1, j2, j3, out_ref):
    rows = jnp.concatenate([j[...].astype(f32) for j in (j0, j3, j2, j1)], axis=0)
    b = transposed(rows)
    out_ref[0:32, :] = pltpu.roll(jnp.concatenate([b, b], axis=1), lax.axis_index("ia") * 16, 1)
    rows = jnp.concatenate([rows, rows, jnp.zeros((64, 128 - 2 * R), f32)], axis=1)
    turned = [pltpu.roll(rows, 128 - d, 1) if d else rows for d in range(DIAGONALS)]
    diagonals = [jnp.sum(rows * x, axis=0, keepdims=True) for x in turned]
    diagonals = pad_rows(jnp.concatenate(diagonals, axis=0), 16)
    low = lanes_of((8, 128)) < 32
    out_ref[32:40, :] = jnp.where(low, diagonals[0:8], pltpu.roll(diagonals[8:16], 32, 1))


def part_copy(t_ref, dst, s, sem):
    dest = lax.rem(lax.axis_index("ka") + s, 4)
    block = t_ref.at[:, pl.ds(pl.multiple_of(dest * 64, 64), 64), :]
    return pltpu.make_async_copy(block, dst, sem)


def load_kernel(t_ref, out_ref, sem):
    copy = part_copy(t_ref, out_ref, 2, sem)
    copy.start()
    copy.wait()


def contract_kernel(c_ref, part_ref, t_ref, *refs):
    msgs, held_ref, sems = refs[0:4], refs[4], refs[5]
    copies = {s: part_copy(t_ref, held_ref.at[n], s, sems.at[n]) for n, s in enumerate((1, 3, 0))}
    for copy in copies.values():
        copy.start()
    blocks = [c_ref[p].astype(f32) for p in range(16)]
    low = lanes_of((16, 128)) < 64
    tops, bottoms = [], []
    for a, b in zip(blocks[0::2], blocks[1::2]):
        tops.append(jnp.where(low, a, pltpu.roll(b, 64, 1)))
        bottoms.append(jnp.where(low, pltpu.roll(a, 64, 1), b))
    c = jnp.concatenate([jnp.concatenate(tops, axis=1), jnp.concatenate(bottoms, axis=1)], axis=0).astype(bf16)
    nt = (((1,), (1,)), ((), ()))
    gram = fold(lax.dot_general(c, c, nt, preferred_element_type=f32))
    for s in (2, 1, 3, 0):
        if s in copies:
            copies[s].wait()
        block = held_ref[(1, 3, 0).index(s)] if s in copies else part_ref[...]
        y = lax.dot_general(c, block.reshape(1024, 1024), nt, preferred_element_type=f32)
        for t in range(TILES):
            msgs[s][24 * t : 24 * t + 24, :] = y[0:24, 128 * t : 128 * t + 128]
            msgs[s][192 + t : 193 + t, :] = y[24:25, 128 * t : 128 * t + 128]
        msgs[s][BODY:MSG, :] = gram


def partial_kernel(y0, y1, y2, y3, b0, b1, b2, b3, pay_ref):
    ys, bs = (y0, y1, y2, y3), (b0, b1, b2, b3)
    lane24, low24 = lanes_of((24, 128)), lanes_of((24, 128)) < 64
    m = jnp.zeros((24, 128), f32)
    for t in range(TILES):
        at = slice(24 * t, 24 * t + 24)
        p = functools.reduce(jnp.add, [y[at, :] * b[0:24, :] for y, b in zip(ys, bs)])
        m = jnp.where(lane24 == 2 * t, jnp.sum(jnp.where(low24, p, 0.0), axis=1, keepdims=True), m)
        m = jnp.where(lane24 == 2 * t + 1, jnp.sum(jnp.where(low24, 0.0, p), axis=1, keepdims=True), m)
    p = functools.reduce(jnp.add, [y[192:200, :] * b[24:25, :] for y, b in zip(ys, bs)])
    low8 = lanes_of((8, 128)) < 64
    last = [jnp.sum(jnp.where(keep, p, 0.0), axis=1, keepdims=True) for keep in (low8, ~low8)]
    d = (b0[32:40, :] + b1[32:40, :]) + (b2[32:40, :] + b3[32:40, :])
    d = jnp.concatenate([d[:, 0:32], d[:, 32:64]], axis=0)
    d = pltpu.roll(d, lax.rem(16 - 4 * lax.axis_index("ka"), 16), 0)[0:4, 0:R]
    pay = [m[4 * q : 4 * q + 4, 0:16] for q in range(6)] + [d]
    pay += [x[v : v + 4] for v in (0, 4) for x in last] + [jnp.zeros((4, 3), f32)]
    pay_ref[...] = jnp.broadcast_to(jnp.concatenate(pay, axis=1)[None], pay_ref.shape)


def sum_kernel(y0, y1, y2, y3, y_ref, gk_ref):
    def total(at):
        return (y0[at, :] + y1[at, :]) + (y2[at, :] + y3[at, :])

    for t in range(TILES):
        s = total(slice(24 * t, 24 * t + 24))
        y_ref[pl.ds(2 * t, 24, stride=16), :] = s[:, 0:64]
        y_ref[pl.ds(2 * t + 1, 24, stride=16), :] = s[:, 64:128]
    s = total(slice(192, 200))
    y_ref[pl.ds(384, 8, stride=2), :] = s[:, 0:64]
    y_ref[pl.ds(385, 8, stride=2), :] = s[:, 64:128]
    gk_ref[...] = total(slice(BODY, MSG))


def solve_kernel(x_ref, gk_ref, out_ref):
    x = jnp.sum(x_ref[...].reshape(16, 4, 4, 128), axis=0)
    d = jnp.concatenate([x[q][:, 96 : 96 + R] for q in range(4)], axis=0)
    x = (x[0] + x[1]) + (x[2] + x[3])
    lane, sub = lanes_of((4, 16)), sublanes_of((4, 16))
    last = jnp.zeros((4, 16), f32)
    for q in range(4):
        here = (lane // 8 == q // 2) & (lane % 2 == q % 2) & (lane // 2 % 4 == sub)
        last = jnp.where(here, x[:, 121 + q : 122 + q], last)
    last = jnp.sum(last, axis=0, keepdims=True)
    m = pad_rows(jnp.concatenate([x[:, 16 * q : 16 * q + 16] for q in range(6)] + [last], axis=0), 32)
    row, lane = sublanes_of((32, 32)), lanes_of((32, 32))
    d = jnp.concatenate([d, jnp.zeros((16, 32 - R), f32)], axis=1)
    apart = jnp.where(row < lane, row - lane + R, row - lane)
    gram = jnp.zeros((32, 32), f32)
    for q in range(1, DIAGONALS):
        gram = jnp.where(apart == q, d[q : q + 1, :], gram)
    gram = gram + transposed(gram)
    gram = jnp.where(apart == 0, d[0:1, :], gram)
    n = jnp.where((row < R) & (lane < R), gram * unfold(gk_ref[...]), 0.0)
    a = jnp.concatenate([n, m, jnp.zeros((32, 80), f32)], axis=1)
    row_at = sublanes_of((32, 128))
    for first in range(0, R, BLOCK):
        cols = [jnp.broadcast_to(a[:, p : p + 1], (32, 128)) for p in range(first, min(first + BLOCK, R))]
        for q in range(len(cols)):
            p = first + q
            scale = 1.0 / cols[q][p : p + 1, :]

            def eliminate(x):
                row = jnp.broadcast_to(x[p : p + 1, :] * scale, (32, 128))
                return jnp.where(row_at == p, row, x - cols[q] * row)

            a = eliminate(a)
            cols[q + 1 :] = [eliminate(x) for x in cols[q + 1 :]]
    out_ref[...] = pad_rows(a, 128).T[32:48, 0:R]


def call(kernel, out, specs, flops=0, nbytes=0, scratch=()):
    return pl.pallas_call(
        kernel,
        out_shape=out,
        in_specs=specs,
        out_specs=jax.tree.map(lambda _: VM, out),
        scratch_shapes=scratch,
        compiler_params=pltpu.CompilerParams(vmem_limit_bytes=10 * 2**20),
        cost_estimate=pl.CostEstimate(flops=flops, bytes_accessed=nbytes, transcendentals=0),
    )


def shift(x, axis, by, n):
    return lax.ppermute(x, axis, [(i, (i + by) % n) for i in range(n)])


def per_device(tensor, factor_j, factor_k):
    sds = jax.ShapeDtypeStruct
    dma = pltpu.SemaphoreType.DMA
    factor_k = pltpu.with_memory_space_constraint(factor_k, pltpu.HBM)
    tensor = pltpu.with_memory_space_constraint(tensor, pltpu.HBM)
    j0 = factor_j.T
    js = [shift(j0, "ia", s, 4) for s in (1, 2, 3)]
    packed = call(pack_kernel, sds((16, 16, 128), bf16), [HB], scratch=[pltpu.VMEM((R, 64), bf16), dma(())])(factor_k)
    c = lax.all_to_all(packed, ("z", "c"), 0, 0, tiled=True)
    part = call(load_kernel, sds((16, 64, 1024), bf16), [HB], 0, 2**22, [dma(())])(tensor)
    part = pltpu.with_memory_space_constraint(part, pltpu.VMEM)
    b = call(factor_kernel, sds((40, 128), f32), [VM] * 4, 2**33, 2**20)(j0, *js)
    bs = [b] + [shift(b, "ka", 4 - s, 4) for s in (1, 2, 3)]
    msgs = call(
        contract_kernel, [sds((MSG, 128), f32)] * 4, [VM, VM, HB], 2**34, 2**23,
        [pltpu.VMEM((3, 16, 64, 1024), bf16), dma((3,))],
    )(c, part, tensor)
    got = [shift(msgs[s], "ka", s, 4) for s in (1, 2, 3)]
    pay = call(partial_kernel, sds((64, 4, 128), f32), [VM] * 8)(*msgs, *bs)
    pay = lax.all_to_all(pay, ("z", "c", "ka"), 0, 0, tiled=True)
    y, gram_k = call(sum_kernel, [sds((400, 64), f32), sds((8, 128), f32)], [VM] * 4, 0, 2**21)(msgs[0], *got)
    new_factor = call(solve_kernel, sds((16, R), f32), [VM] * 2)(pay, gram_k)
    return y.reshape(R, 16, 64), new_factor.T


def solution(mesh):
    ia, ja, ka = (mesh.shape[a] for a in ("ia", "ja", "ka"))
    mesh = jax.sharding.Mesh(mesh.devices.reshape(ia, ja // 2, 2, ka), ("ia", "z", "c", "ka"))
    in_specs = (P("ia", ("z", "c"), "ka"), P(None, ("z", "c", "ka", "ia")), P(None, ("ka", "z", "c")))
    out_specs = (P(None, "ia", ("z", "c", "ka")), P(None, "ia"))
    return jax.shard_map(
        per_device, mesh=mesh, in_specs=in_specs, out_specs=out_specs, check_vma=False
    )
```

```python
import functools

import jax
import jax.numpy as jnp
from jax import lax
from jax.experimental import pallas as pl
from jax.experimental.pallas import tpu as pltpu
from jax.sharding import PartitionSpec as P

f32, bf16 = jnp.float32, jnp.bfloat16
R = 25
VM = pl.BlockSpec(memory_space=pltpu.VMEM)
HB = pl.BlockSpec(memory_space=pltpu.HBM)
TILES, BODY, MSG = 8, 200, 208
DIAGONALS = 13
BLOCK = 13


def lanes_of(shape):
    return lax.broadcasted_iota(jnp.int32, shape, 1)


def sublanes_of(shape):
    return lax.broadcasted_iota(jnp.int32, shape, 0)


def pad_rows(x, rows):
    return jnp.concatenate([x, jnp.zeros((rows - x.shape[0], x.shape[1]), x.dtype)], axis=0)


def fold(g):
    return jnp.concatenate([g[8 * q : 8 * q + 8] for q in range(4)], axis=1)


def unfold(g):
    return jnp.concatenate([g[:, 32 * q : 32 * q + 32] for q in range(4)], axis=0)


def transposed(x):
    rows = -(-x.shape[1] // 8) * 8
    x = jnp.concatenate([x, jnp.zeros((x.shape[0], 128 - x.shape[1]), x.dtype)], axis=1)
    return pad_rows(x, 128).T[0:rows, 0 : x.shape[0]]


def pack_kernel(k_ref, out_ref, k_vmem, sem):
    copy = pltpu.make_async_copy(k_ref, k_vmem, sem)
    copy.start()
    copy.wait()
    k = pad_rows(k_vmem[...].astype(f32), 32)
    folded = jnp.concatenate([k[0:16], k[16:32]], axis=1).astype(bf16)
    out_ref[...] = jnp.broadcast_to(folded[None], out_ref.shape)


def factor_kernel(j0, j1, j2, j3, out_ref):
    rows = jnp.concatenate([j[...].astype(f32) for j in (j0, j3, j2, j1)], axis=0)
    b = transposed(rows)
    out_ref[0:32, :] = pltpu.roll(jnp.concatenate([b, b], axis=1), lax.axis_index("ia") * 16, 1)
    rows = jnp.concatenate([rows, rows, jnp.zeros((64, 128 - 2 * R), f32)], axis=1)
    turned = [pltpu.roll(rows, 128 - d, 1) if d else rows for d in range(DIAGONALS)]
    diagonals = [jnp.sum(rows * x, axis=0, keepdims=True) for x in turned]
    diagonals = pad_rows(jnp.concatenate(diagonals, axis=0), 16)
    low = lanes_of((8, 128)) < 32
    out_ref[32:40, :] = jnp.where(low, diagonals[0:8], pltpu.roll(diagonals[8:16], 32, 1))


def part_copy(t_ref, dst, s, sem):
    dest = lax.rem(lax.axis_index("ka") + s, 4)
    block = t_ref.at[:, pl.ds(pl.multiple_of(dest * 64, 64), 64), :]
    return pltpu.make_async_copy(block, dst, sem)


ORDER = (2, 1, 3, 0)


def contract_kernel(c_ref, t_ref, *refs):
    msgs, held_ref, sems = refs[0:4], refs[4], refs[5]
    copies = [part_copy(t_ref, held_ref.at[s], s, sems.at[s]) for s in range(4)]
    for s in ORDER:
        copies[s].start()
    blocks = [c_ref[p].astype(f32) for p in range(16)]
    low = lanes_of((16, 128)) < 64
    tops, bottoms = [], []
    for a, b in zip(blocks[0::2], blocks[1::2]):
        tops.append(jnp.where(low, a, pltpu.roll(b, 64, 1)))
        bottoms.append(jnp.where(low, pltpu.roll(a, 64, 1), b))
    c = jnp.concatenate([jnp.concatenate(tops, axis=1), jnp.concatenate(bottoms, axis=1)], axis=0).astype(bf16)
    nt = (((1,), (1,)), ((), ()))
    gram = fold(lax.dot_general(c, c, nt, preferred_element_type=f32))
    for s in ORDER:
        copies[s].wait()
        y = lax.dot_general(c, held_ref[s].reshape(1024, 1024), nt, preferred_element_type=f32)
        for t in range(TILES):
            msgs[s][24 * t : 24 * t + 24, :] = y[0:24, 128 * t : 128 * t + 128]
            msgs[s][192 + t : 193 + t, :] = y[24:25, 128 * t : 128 * t + 128]
        msgs[s][BODY:MSG, :] = gram


def partial_kernel(y0, y1, y2, y3, b0, b1, b2, b3, pay_ref):
    ys, bs = (y0, y1, y2, y3), (b0, b1, b2, b3)
    lane24, low24 = lanes_of((24, 128)), lanes_of((24, 128)) < 64
    m = jnp.zeros((24, 128), f32)
    for t in range(TILES):
        at = slice(24 * t, 24 * t + 24)
        p = functools.reduce(jnp.add, [y[at, :] * b[0:24, :] for y, b in zip(ys, bs)])
        m = jnp.where(lane24 == 2 * t, jnp.sum(jnp.where(low24, p, 0.0), axis=1, keepdims=True), m)
        m = jnp.where(lane24 == 2 * t + 1, jnp.sum(jnp.where(low24, 0.0, p), axis=1, keepdims=True), m)
    p = functools.reduce(jnp.add, [y[192:200, :] * b[24:25, :] for y, b in zip(ys, bs)])
    low8 = lanes_of((8, 128)) < 64
    last = [jnp.sum(jnp.where(keep, p, 0.0), axis=1, keepdims=True) for keep in (low8, ~low8)]
    d = (b0[32:40, :] + b1[32:40, :]) + (b2[32:40, :] + b3[32:40, :])
    d = jnp.concatenate([d[:, 0:32], d[:, 32:64]], axis=0)
    d = pltpu.roll(d, lax.rem(16 - 4 * lax.axis_index("ka"), 16), 0)[0:4, 0:R]
    pay = [m[4 * q : 4 * q + 4, 0:16] for q in range(6)] + [d]
    pay += [x[v : v + 4] for v in (0, 4) for x in last] + [jnp.zeros((4, 3), f32)]
    pay_ref[...] = jnp.broadcast_to(jnp.concatenate(pay, axis=1)[None], pay_ref.shape)


def finish_kernel(y0, y1, y2, y3, x_ref, y_ref, out_ref, held_ref, sem):
    def total(at):
        return (y0[at, :] + y1[at, :]) + (y2[at, :] + y3[at, :])

    for t in range(TILES):
        s = total(slice(24 * t, 24 * t + 24))
        held_ref[pl.ds(2 * t, 24, stride=16), :] = s[:, 0:64]
        held_ref[pl.ds(2 * t + 1, 24, stride=16), :] = s[:, 64:128]
    s = total(slice(192, 200))
    held_ref[pl.ds(384, 8, stride=2), :] = s[:, 0:64]
    held_ref[pl.ds(385, 8, stride=2), :] = s[:, 64:128]
    copy = pltpu.make_async_copy(held_ref, y_ref, sem)
    copy.start()
    gram_k = unfold(total(slice(BODY, MSG)))
    x = jnp.sum(x_ref[...].reshape(16, 4, 4, 128), axis=0)
    d = jnp.concatenate([x[q][:, 96 : 96 + R] for q in range(4)], axis=0)
    x = (x[0] + x[1]) + (x[2] + x[3])
    lane, sub = lanes_of((4, 16)), sublanes_of((4, 16))
    last = jnp.zeros((4, 16), f32)
    for q in range(4):
        here = (lane // 8 == q // 2) & (lane % 2 == q % 2) & (lane // 2 % 4 == sub)
        last = jnp.where(here, x[:, 121 + q : 122 + q], last)
    last = jnp.sum(last, axis=0, keepdims=True)
    m = pad_rows(jnp.concatenate([x[:, 16 * q : 16 * q + 16] for q in range(6)] + [last], axis=0), 32)
    row, lane = sublanes_of((32, 32)), lanes_of((32, 32))
    d = jnp.concatenate([d, jnp.zeros((16, 32 - R), f32)], axis=1)
    apart = jnp.where(row < lane, row - lane + R, row - lane)
    gram = jnp.zeros((32, 32), f32)
    for q in range(1, DIAGONALS):
        gram = jnp.where(apart == q, d[q : q + 1, :], gram)
    gram = gram + transposed(gram)
    gram = jnp.where(apart == 0, d[0:1, :], gram)
    n = jnp.where((row < R) & (lane < R), gram * gram_k, 0.0)
    a = jnp.concatenate([n, m, jnp.zeros((32, 80), f32)], axis=1)
    row_at = sublanes_of((32, 128))
    for first in range(0, R, BLOCK):
        cols = [jnp.broadcast_to(a[:, p : p + 1], (32, 128)) for p in range(first, min(first + BLOCK, R))]
        for q in range(len(cols)):
            p = first + q
            scale = 1.0 / cols[q][p : p + 1, :]

            def eliminate(x):
                row = jnp.broadcast_to(x[p : p + 1, :] * scale, (32, 128))
                return jnp.where(row_at == p, row, x - cols[q] * row)

            a = eliminate(a)
            cols[q + 1 :] = [eliminate(x) for x in cols[q + 1 :]]
    out_ref[...] = pad_rows(a, 128).T[32:48, 0:R]
    copy.wait()


def call(kernel, out, specs, flops=0, nbytes=0, scratch=(), out_specs=None):
    return pl.pallas_call(
        kernel,
        out_shape=out,
        in_specs=specs,
        out_specs=out_specs or jax.tree.map(lambda _: VM, out),
        scratch_shapes=scratch,
        compiler_params=pltpu.CompilerParams(vmem_limit_bytes=12 * 2**20),
        cost_estimate=pl.CostEstimate(flops=flops, bytes_accessed=nbytes, transcendentals=0),
    )


def shift(x, axis, by, n):
    return lax.ppermute(x, axis, [(i, (i + by) % n) for i in range(n)])


def per_device(tensor, factor_j, factor_k):
    sds = jax.ShapeDtypeStruct
    dma = pltpu.SemaphoreType.DMA
    factor_k = pltpu.with_memory_space_constraint(factor_k, pltpu.HBM)
    tensor = pltpu.with_memory_space_constraint(tensor, pltpu.HBM)
    j0 = factor_j.T
    js = [shift(j0, "ia", s, 4) for s in (1, 2, 3)]
    packed = call(pack_kernel, sds((16, 16, 128), bf16), [HB], scratch=[pltpu.VMEM((R, 64), bf16), dma(())])(factor_k)
    c = lax.all_to_all(packed, ("z", "c"), 0, 0, tiled=True)
    b = call(factor_kernel, sds((40, 128), f32), [VM] * 4, 2**33, 2**20)(j0, *js)
    bs = [b] + [shift(b, "ka", 4 - s, 4) for s in (1, 2, 3)]
    msgs = call(
        contract_kernel, [sds((MSG, 128), f32)] * 4, [VM, HB], 2**34, 2**23,
        [pltpu.VMEM((4, 16, 64, 1024), bf16), dma((4,))],
    )(c, tensor)
    got = [shift(msgs[s], "ka", s, 4) for s in (1, 2, 3)]
    pay = call(partial_kernel, sds((64, 4, 128), f32), [VM] * 8)(*msgs, *bs)
    pay = lax.all_to_all(pay, ("z", "c", "ka"), 0, 0, tiled=True)
    y, new_factor = call(
        finish_kernel, [sds((400, 64), f32), sds((16, R), f32)], [VM] * 5, 0, 0,
        [pltpu.VMEM((400, 64), f32), dma(())], [HB, VM],
    )(msgs[0], *got, pay)
    return y.reshape(R, 16, 64), new_factor.T


def solution(mesh):
    ia, ja, ka = (mesh.shape[a] for a in ("ia", "ja", "ka"))
    mesh = jax.sharding.Mesh(mesh.devices.reshape(ia, ja // 2, 2, ka), ("ia", "z", "c", "ka"))
    in_specs = (P("ia", ("z", "c"), "ka"), P(None, ("z", "c", "ka", "ia")), P(None, ("ka", "z", "c")))
    out_specs = (P(None, "ia", ("z", "c", "ka")), P(None, "ia"))
    return jax.shard_map(
        per_device, mesh=mesh, in_specs=in_specs, out_specs=out_specs, check_vma=False
    )
```

```python
import functools

import jax
import jax.numpy as jnp
from jax import lax
from jax.experimental import pallas as pl
from jax.experimental.pallas import tpu as pltpu
from jax.sharding import PartitionSpec as P

f32, bf16 = jnp.float32, jnp.bfloat16
R = 25
VM = pl.BlockSpec(memory_space=pltpu.VMEM)
HB = pl.BlockSpec(memory_space=pltpu.HBM)
TILES, BODY, MSG = 8, 200, 208
DIAGONALS = 13
BLOCK = 13


def lanes_of(shape):
    return lax.broadcasted_iota(jnp.int32, shape, 1)


def sublanes_of(shape):
    return lax.broadcasted_iota(jnp.int32, shape, 0)


def pad_rows(x, rows):
    return jnp.concatenate([x, jnp.zeros((rows - x.shape[0], x.shape[1]), x.dtype)], axis=0)


def fold(g):
    return jnp.concatenate([g[8 * q : 8 * q + 8] for q in range(4)], axis=1)


def unfold(g):
    return jnp.concatenate([g[:, 32 * q : 32 * q + 32] for q in range(4)], axis=0)


def transposed(x):
    rows = -(-x.shape[1] // 8) * 8
    x = jnp.concatenate([x, jnp.zeros((x.shape[0], 128 - x.shape[1]), x.dtype)], axis=1)
    return pad_rows(x, 128).T[0:rows, 0 : x.shape[0]]


def own_kernel(k_ref, j_ref, kout_ref, jout_ref, sems):
    copies = [pltpu.make_async_copy(k_ref, kout_ref, sems.at[0]), pltpu.make_async_copy(j_ref, jout_ref, sems.at[1])]
    for copy in copies:
        copy.start()
    for copy in copies:
        copy.wait()


def pack_kernel(k_ref, out_ref):
    k = pad_rows(k_ref[...].astype(f32), 32)
    folded = jnp.concatenate([k[0:16], k[16:32]], axis=1).astype(bf16)
    out_ref[...] = jnp.broadcast_to(folded[None], out_ref.shape)


def factor_kernel(j0, j1, j2, j3, out_ref):
    rows = jnp.concatenate([j[...].astype(f32) for j in (j0, j3, j2, j1)], axis=0)
    b = transposed(rows)
    out_ref[0:32, :] = pltpu.roll(jnp.concatenate([b, b], axis=1), lax.axis_index("ia") * 16, 1)
    rows = jnp.concatenate([rows, rows, jnp.zeros((64, 128 - 2 * R), f32)], axis=1)
    turned = [pltpu.roll(rows, 128 - d, 1) if d else rows for d in range(DIAGONALS)]
    diagonals = [jnp.sum(rows * x, axis=0, keepdims=True) for x in turned]
    diagonals = pad_rows(jnp.concatenate(diagonals, axis=0), 16)
    low = lanes_of((8, 128)) < 32
    out_ref[32:40, :] = jnp.where(low, diagonals[0:8], pltpu.roll(diagonals[8:16], 32, 1))


def part_copy(t_ref, dst, s, sem):
    dest = lax.rem(lax.axis_index("ka") + s, 4)
    block = t_ref.at[:, pl.ds(pl.multiple_of(dest * 64, 64), 64), :]
    return pltpu.make_async_copy(block, dst, sem)


ORDER = (2, 1, 3, 0)


def contract_kernel(c_ref, t_ref, *refs):
    msgs, held_ref, sems = refs[0:4], refs[4], refs[5]
    copies = [part_copy(t_ref, held_ref.at[s], s, sems.at[s]) for s in range(4)]
    for s in ORDER:
        copies[s].start()
    blocks = [c_ref[p].astype(f32) for p in range(16)]
    low = lanes_of((16, 128)) < 64
    tops, bottoms = [], []
    for a, b in zip(blocks[0::2], blocks[1::2]):
        tops.append(jnp.where(low, a, pltpu.roll(b, 64, 1)))
        bottoms.append(jnp.where(low, pltpu.roll(a, 64, 1), b))
    c = jnp.concatenate([jnp.concatenate(tops, axis=1), jnp.concatenate(bottoms, axis=1)], axis=0).astype(bf16)
    nt = (((1,), (1,)), ((), ()))
    gram = fold(lax.dot_general(c, c, nt, preferred_element_type=f32))
    for s in ORDER:
        copies[s].wait()
        y = lax.dot_general(c, held_ref[s].reshape(1024, 1024), nt, preferred_element_type=f32)
        for t in range(TILES):
            msgs[s][24 * t : 24 * t + 24, :] = y[0:24, 128 * t : 128 * t + 128]
            msgs[s][192 + t : 193 + t, :] = y[24:25, 128 * t : 128 * t + 128]
        msgs[s][BODY:MSG, :] = gram


def partial_kernel(y0, y1, y2, y3, b0, b1, b2, b3, pay_ref):
    ys, bs = (y0, y1, y2, y3), (b0, b1, b2, b3)
    lane24, low24 = lanes_of((24, 128)), lanes_of((24, 128)) < 64
    m = jnp.zeros((24, 128), f32)
    for t in range(TILES):
        at = slice(24 * t, 24 * t + 24)
        p = functools.reduce(jnp.add, [y[at, :] * b[0:24, :] for y, b in zip(ys, bs)])
        m = jnp.where(lane24 == 2 * t, jnp.sum(jnp.where(low24, p, 0.0), axis=1, keepdims=True), m)
        m = jnp.where(lane24 == 2 * t + 1, jnp.sum(jnp.where(low24, 0.0, p), axis=1, keepdims=True), m)
    p = functools.reduce(jnp.add, [y[192:200, :] * b[24:25, :] for y, b in zip(ys, bs)])
    low8 = lanes_of((8, 128)) < 64
    last = [jnp.sum(jnp.where(keep, p, 0.0), axis=1, keepdims=True) for keep in (low8, ~low8)]
    d = (b0[32:40, :] + b1[32:40, :]) + (b2[32:40, :] + b3[32:40, :])
    d = jnp.concatenate([d[:, 0:32], d[:, 32:64]], axis=0)
    d = pltpu.roll(d, lax.rem(16 - 4 * lax.axis_index("ka"), 16), 0)[0:4, 0:R]
    pay = [m[4 * q : 4 * q + 4, 0:16] for q in range(6)] + [d]
    pay += [x[v : v + 4] for v in (0, 4) for x in last] + [jnp.zeros((4, 3), f32)]
    pay_ref[...] = jnp.broadcast_to(jnp.concatenate(pay, axis=1)[None], pay_ref.shape)


def finish_kernel(y0, y1, y2, y3, x_ref, y_ref, out_ref, held_ref, sem):
    def total(at):
        return (y0[at, :] + y1[at, :]) + (y2[at, :] + y3[at, :])

    for t in range(TILES):
        s = total(slice(24 * t, 24 * t + 24))
        held_ref[pl.ds(2 * t, 24, stride=16), :] = s[:, 0:64]
        held_ref[pl.ds(2 * t + 1, 24, stride=16), :] = s[:, 64:128]
    s = total(slice(192, 200))
    held_ref[pl.ds(384, 8, stride=2), :] = s[:, 0:64]
    held_ref[pl.ds(385, 8, stride=2), :] = s[:, 64:128]
    copy = pltpu.make_async_copy(held_ref, y_ref, sem)
    copy.start()
    gram_k = unfold(total(slice(BODY, MSG)))
    x = jnp.sum(x_ref[...].reshape(16, 4, 4, 128), axis=0)
    d = jnp.concatenate([x[q][:, 96 : 96 + R] for q in range(4)], axis=0)
    x = (x[0] + x[1]) + (x[2] + x[3])
    lane, sub = lanes_of((4, 16)), sublanes_of((4, 16))
    last = jnp.zeros((4, 16), f32)
    for q in range(4):
        here = (lane // 8 == q // 2) & (lane % 2 == q % 2) & (lane // 2 % 4 == sub)
        last = jnp.where(here, x[:, 121 + q : 122 + q], last)
    last = jnp.sum(last, axis=0, keepdims=True)
    m = pad_rows(jnp.concatenate([x[:, 16 * q : 16 * q + 16] for q in range(6)] + [last], axis=0), 32)
    row, lane = sublanes_of((32, 32)), lanes_of((32, 32))
    d = jnp.concatenate([d, jnp.zeros((16, 32 - R), f32)], axis=1)
    apart = jnp.where(row < lane, row - lane + R, row - lane)
    gram = jnp.zeros((32, 32), f32)
    for q in range(1, DIAGONALS):
        gram = jnp.where(apart == q, d[q : q + 1, :], gram)
    gram = gram + transposed(gram)
    gram = jnp.where(apart == 0, d[0:1, :], gram)
    n = jnp.where((row < R) & (lane < R), gram * gram_k, 0.0)
    a = jnp.concatenate([n, m, jnp.zeros((32, 80), f32)], axis=1)
    row_at = sublanes_of((32, 128))
    for first in range(0, R, BLOCK):
        cols = [jnp.broadcast_to(a[:, p : p + 1], (32, 128)) for p in range(first, min(first + BLOCK, R))]
        for q in range(len(cols)):
            p = first + q
            scale = 1.0 / cols[q][p : p + 1, :]

            def eliminate(x):
                row = jnp.broadcast_to(x[p : p + 1, :] * scale, (32, 128))
                return jnp.where(row_at == p, row, x - cols[q] * row)

            a = eliminate(a)
            cols[q + 1 :] = [eliminate(x) for x in cols[q + 1 :]]
    out_ref[...] = pad_rows(a, 128).T[32:48, 0:R]
    copy.wait()


def call(kernel, out, specs, flops=0, nbytes=0, scratch=(), out_specs=None):
    return pl.pallas_call(
        kernel,
        out_shape=out,
        in_specs=specs,
        out_specs=out_specs or jax.tree.map(lambda _: VM, out),
        scratch_shapes=scratch,
        compiler_params=pltpu.CompilerParams(vmem_limit_bytes=12 * 2**20),
        cost_estimate=pl.CostEstimate(flops=flops, bytes_accessed=nbytes, transcendentals=0),
    )


def shift(x, axis, by, n):
    return lax.ppermute(x, axis, [(i, (i + by) % n) for i in range(n)])


def per_device(tensor, factor_j, factor_k):
    sds = jax.ShapeDtypeStruct
    dma = pltpu.SemaphoreType.DMA
    factor_k = pltpu.with_memory_space_constraint(factor_k, pltpu.HBM)
    tensor = pltpu.with_memory_space_constraint(tensor, pltpu.HBM)
    j0 = factor_j.T
    js = [shift(j0, "ia", s, 4) for s in (1, 2, 3)]
    k_own, j_own = call(
        own_kernel, [sds((R, 64), bf16), sds((16, R), bf16)], [HB, HB], 0, 0, [dma((2,))]
    )(factor_k, pltpu.with_memory_space_constraint(j0, pltpu.HBM))
    packed = call(pack_kernel, sds((16, 16, 128), bf16), [VM])(k_own)
    c = lax.all_to_all(packed, ("z", "c"), 0, 0, tiled=True)
    b = call(factor_kernel, sds((40, 128), f32), [VM] * 4, 2**33, 2**20)(j_own, *js)
    bs = [b] + [shift(b, "ka", 4 - s, 4) for s in (1, 2, 3)]
    msgs = call(
        contract_kernel, [sds((MSG, 128), f32)] * 4, [VM, HB], 2**34, 2**23,
        [pltpu.VMEM((4, 16, 64, 1024), bf16), dma((4,))],
    )(c, tensor)
    got = {s: shift(msgs[s], "ka", s, 4) for s in (2, 1, 3)}
    pay = call(partial_kernel, sds((64, 4, 128), f32), [VM] * 8)(*msgs, *bs)
    pay = lax.all_to_all(pay, ("z", "c", "ka"), 0, 0, tiled=True)
    y, new_factor = call(
        finish_kernel, [sds((400, 64), f32), sds((16, R), f32)], [VM] * 5, 0, 0,
        [pltpu.VMEM((400, 64), f32), dma(())], [HB, VM],
    )(msgs[0], got[2], got[1], got[3], pay)
    return y.reshape(R, 16, 64), new_factor.T


def solution(mesh):
    ia, ja, ka = (mesh.shape[a] for a in ("ia", "ja", "ka"))
    mesh = jax.sharding.Mesh(mesh.devices.reshape(ia, ja // 2, 2, ka), ("ia", "z", "c", "ka"))
    in_specs = (P("ia", ("z", "c"), "ka"), P(None, ("z", "c", "ka", "ia")), P(None, ("ka", "z", "c")))
    out_specs = (P(None, "ia", ("z", "c", "ka")), P(None, "ia"))
    return jax.shard_map(
        per_device, mesh=mesh, in_specs=in_specs, out_specs=out_specs, check_vma=False
    )
```

```python
import functools

import jax
import jax.numpy as jnp
from jax import lax
from jax.experimental import pallas as pl
from jax.experimental.pallas import tpu as pltpu
from jax.sharding import PartitionSpec as P

f32, bf16 = jnp.float32, jnp.bfloat16
R = 25
VM = pl.BlockSpec(memory_space=pltpu.VMEM)
HB = pl.BlockSpec(memory_space=pltpu.HBM)
TILES, BODY, MSG = 8, 200, 208
DIAGONALS = 13
BLOCK = 13


def lanes_of(shape):
    return lax.broadcasted_iota(jnp.int32, shape, 1)


def sublanes_of(shape):
    return lax.broadcasted_iota(jnp.int32, shape, 0)


def pad_rows(x, rows):
    return jnp.concatenate([x, jnp.zeros((rows - x.shape[0], x.shape[1]), x.dtype)], axis=0)


def fold(g):
    return jnp.concatenate([g[8 * q : 8 * q + 8] for q in range(4)], axis=1)


def unfold(g):
    return jnp.concatenate([g[:, 32 * q : 32 * q + 32] for q in range(4)], axis=0)


def transposed(x):
    rows = -(-x.shape[1] // 8) * 8
    x = jnp.concatenate([x, jnp.zeros((x.shape[0], 128 - x.shape[1]), x.dtype)], axis=1)
    return pad_rows(x, 128).T[0:rows, 0 : x.shape[0]]


def own_kernel(k_ref, j_ref, kout_ref, jout_ref, sems):
    copies = [pltpu.make_async_copy(k_ref, kout_ref, sems.at[0]), pltpu.make_async_copy(j_ref, jout_ref, sems.at[1])]
    for copy in copies:
        copy.start()
    for copy in copies:
        copy.wait()


def pack_kernel(k_ref, out_ref):
    k = pad_rows(k_ref[...].astype(f32), 32)
    folded = jnp.concatenate([k[0:16], k[16:32]], axis=1).astype(bf16)
    out_ref[...] = jnp.broadcast_to(folded[None], out_ref.shape)


def factor_kernel(j0, j1, j2, j3, out_ref):
    rows = jnp.concatenate([j[...].astype(f32) for j in (j0, j3, j2, j1)], axis=0)
    b = transposed(rows)
    out_ref[0:32, :] = pltpu.roll(jnp.concatenate([b, b], axis=1), lax.axis_index("ia") * 16, 1)
    rows = jnp.concatenate([rows, rows, jnp.zeros((64, 128 - 2 * R), f32)], axis=1)
    turned = [pltpu.roll(rows, 128 - d, 1) if d else rows for d in range(DIAGONALS)]
    diagonals = [jnp.sum(rows * x, axis=0, keepdims=True) for x in turned]
    diagonals = pad_rows(jnp.concatenate(diagonals, axis=0), 16)
    low = lanes_of((8, 128)) < 32
    out_ref[32:40, :] = jnp.where(low, diagonals[0:8], pltpu.roll(diagonals[8:16], 32, 1))


def part_copy(t_ref, dst, s, sem):
    dest = lax.rem(lax.axis_index("ka") + s, 4)
    block = t_ref.at[:, pl.ds(pl.multiple_of(dest * 64, 64), 64), :]
    return pltpu.make_async_copy(block, dst, sem)


ORDER = (2, 1, 3, 0)


def contract_kernel(c_ref, t_ref, *refs):
    msgs, held_ref, sems = refs[0:4], refs[4], refs[5]
    copies = [part_copy(t_ref, held_ref.at[s], s, sems.at[s]) for s in range(4)]
    for s in ORDER:
        copies[s].start()
    blocks = [c_ref[p].astype(f32) for p in range(16)]
    low = lanes_of((16, 128)) < 64
    tops, bottoms = [], []
    for a, b in zip(blocks[0::2], blocks[1::2]):
        tops.append(jnp.where(low, a, pltpu.roll(b, 64, 1)))
        bottoms.append(jnp.where(low, pltpu.roll(a, 64, 1), b))
    c = jnp.concatenate([jnp.concatenate(tops, axis=1), jnp.concatenate(bottoms, axis=1)], axis=0).astype(bf16)
    nt = (((1,), (1,)), ((), ()))
    gram = fold(lax.dot_general(c, c, nt, preferred_element_type=f32))
    for s in ORDER:
        copies[s].wait()
        y = lax.dot_general(c, held_ref[s].reshape(1024, 1024), nt, preferred_element_type=f32)
        for t in range(TILES):
            msgs[s][24 * t : 24 * t + 24, :] = y[0:24, 128 * t : 128 * t + 128]
            msgs[s][192 + t : 193 + t, :] = y[24:25, 128 * t : 128 * t + 128]
        msgs[s][BODY:MSG, :] = gram


def partial_kernel(y0, y1, y2, y3, b0, b1, b2, b3, pay_ref):
    ys, bs = (y0, y1, y2, y3), (b0, b1, b2, b3)
    lane24, low24 = lanes_of((24, 128)), lanes_of((24, 128)) < 64
    m = jnp.zeros((24, 128), f32)
    for t in range(TILES):
        at = slice(24 * t, 24 * t + 24)
        p = functools.reduce(jnp.add, [y[at, :] * b[0:24, :] for y, b in zip(ys, bs)])
        m = jnp.where(lane24 == 2 * t, jnp.sum(jnp.where(low24, p, 0.0), axis=1, keepdims=True), m)
        m = jnp.where(lane24 == 2 * t + 1, jnp.sum(jnp.where(low24, 0.0, p), axis=1, keepdims=True), m)
    p = functools.reduce(jnp.add, [y[192:200, :] * b[24:25, :] for y, b in zip(ys, bs)])
    low8 = lanes_of((8, 128)) < 64
    last = [jnp.sum(jnp.where(keep, p, 0.0), axis=1, keepdims=True) for keep in (low8, ~low8)]
    d = (b0[32:40, :] + b1[32:40, :]) + (b2[32:40, :] + b3[32:40, :])
    d = jnp.concatenate([d[:, 0:32], d[:, 32:64]], axis=0)
    d = pltpu.roll(d, lax.rem(16 - 4 * lax.axis_index("ka"), 16), 0)[0:4, 0:R]
    pay = [m[4 * q : 4 * q + 4, 0:16] for q in range(6)] + [d]
    pay += [x[v : v + 4] for v in (0, 4) for x in last] + [jnp.zeros((4, 3), f32)]
    pay_ref[...] = jnp.broadcast_to(jnp.concatenate(pay, axis=1)[None], pay_ref.shape)


def add_kernel(x_ref, out_ref):
    out_ref[...] = jnp.sum(x_ref[...].reshape(8, 4, 4, 128), axis=0)


def finish_kernel(y0, y1, y2, y3, x0, x1, y_ref, out_ref, held_ref, sem):
    def total(at):
        return (y0[at, :] + y1[at, :]) + (y2[at, :] + y3[at, :])

    for t in range(TILES):
        s = total(slice(24 * t, 24 * t + 24))
        held_ref[pl.ds(2 * t, 24, stride=16), :] = s[:, 0:64]
        held_ref[pl.ds(2 * t + 1, 24, stride=16), :] = s[:, 64:128]
    s = total(slice(192, 200))
    held_ref[pl.ds(384, 8, stride=2), :] = s[:, 0:64]
    held_ref[pl.ds(385, 8, stride=2), :] = s[:, 64:128]
    copy = pltpu.make_async_copy(held_ref, y_ref, sem)
    copy.start()
    gram_k = unfold(total(slice(BODY, MSG)))
    x = x0[...] + x1[...]
    d = jnp.concatenate([x[q][:, 96 : 96 + R] for q in range(4)], axis=0)
    x = (x[0] + x[1]) + (x[2] + x[3])
    lane, sub = lanes_of((4, 16)), sublanes_of((4, 16))
    last = jnp.zeros((4, 16), f32)
    for q in range(4):
        here = (lane // 8 == q // 2) & (lane % 2 == q % 2) & (lane // 2 % 4 == sub)
        last = jnp.where(here, x[:, 121 + q : 122 + q], last)
    last = jnp.sum(last, axis=0, keepdims=True)
    m = pad_rows(jnp.concatenate([x[:, 16 * q : 16 * q + 16] for q in range(6)] + [last], axis=0), 32)
    row, lane = sublanes_of((32, 32)), lanes_of((32, 32))
    d = jnp.concatenate([d, jnp.zeros((16, 32 - R), f32)], axis=1)
    apart = jnp.where(row < lane, row - lane + R, row - lane)
    gram = jnp.zeros((32, 32), f32)
    for q in range(1, DIAGONALS):
        gram = jnp.where(apart == q, d[q : q + 1, :], gram)
    gram = gram + transposed(gram)
    gram = jnp.where(apart == 0, d[0:1, :], gram)
    n = jnp.where((row < R) & (lane < R), gram * gram_k, 0.0)
    a = jnp.concatenate([n, m, jnp.zeros((32, 80), f32)], axis=1)
    row_at = sublanes_of((32, 128))
    for first in range(0, R, BLOCK):
        cols = [jnp.broadcast_to(a[:, p : p + 1], (32, 128)) for p in range(first, min(first + BLOCK, R))]
        for q in range(len(cols)):
            p = first + q
            scale = 1.0 / cols[q][p : p + 1, :]

            def eliminate(x):
                row = jnp.broadcast_to(x[p : p + 1, :] * scale, (32, 128))
                return jnp.where(row_at == p, row, x - cols[q] * row)

            a = eliminate(a)
            cols[q + 1 :] = [eliminate(x) for x in cols[q + 1 :]]
    out_ref[...] = pad_rows(a, 128).T[32:48, 0:R]
    copy.wait()


def call(kernel, out, specs, flops=0, nbytes=0, scratch=(), out_specs=None):
    return pl.pallas_call(
        kernel,
        out_shape=out,
        in_specs=specs,
        out_specs=out_specs or jax.tree.map(lambda _: VM, out),
        scratch_shapes=scratch,
        compiler_params=pltpu.CompilerParams(vmem_limit_bytes=12 * 2**20),
        cost_estimate=pl.CostEstimate(flops=flops, bytes_accessed=nbytes, transcendentals=0),
    )


def shift(x, axis, by, n):
    return lax.ppermute(x, axis, [(i, (i + by) % n) for i in range(n)])


def per_device(tensor, factor_j, factor_k):
    sds = jax.ShapeDtypeStruct
    dma = pltpu.SemaphoreType.DMA
    factor_k = pltpu.with_memory_space_constraint(factor_k, pltpu.HBM)
    tensor = pltpu.with_memory_space_constraint(tensor, pltpu.HBM)
    j0 = factor_j.T
    js = {s: shift(j0, "ia", s, 4) for s in (1, 3, 2)}
    k_own, j_own = call(
        own_kernel, [sds((R, 64), bf16), sds((16, R), bf16)], [HB, HB], 0, 0, [dma((2,))]
    )(factor_k, pltpu.with_memory_space_constraint(j0, pltpu.HBM))
    packed = call(pack_kernel, sds((16, 16, 128), bf16), [VM])(k_own)
    c = lax.all_to_all(packed, ("z", "c"), 0, 0, tiled=True)
    b = call(factor_kernel, sds((40, 128), f32), [VM] * 4, 2**33, 2**20)(j_own, js[1], js[2], js[3])
    bs = {s: shift(b, "ka", 4 - s, 4) for s in (1, 3, 2)}
    msgs = call(
        contract_kernel, [sds((MSG, 128), f32)] * 4, [VM, HB], 2**34, 2**23,
        [pltpu.VMEM((4, 16, 64, 1024), bf16), dma((4,))],
    )(c, tensor)
    got = {s: shift(msgs[s], "ka", s, 4) for s in (2, 1, 3)}
    pay = call(partial_kernel, sds((32, 4, 128), f32), [VM] * 8)(*msgs, b, bs[1], bs[2], bs[3])
    pay = lax.all_to_all(pay, ("z", "ka"), 0, 0, tiled=True)
    pay = call(add_kernel, sds((4, 4, 128), f32), [VM])(pay)
    other = lax.ppermute(pay, "c", [(0, 1), (1, 0)])
    y, new_factor = call(
        finish_kernel, [sds((400, 64), f32), sds((16, R), f32)], [VM] * 6, 0, 0,
        [pltpu.VMEM((400, 64), f32), dma(())], [HB, VM],
    )(msgs[0], got[2], got[1], got[3], pay, other)
    return y.reshape(R, 16, 64), new_factor.T


def solution(mesh):
    ia, ja, ka = (mesh.shape[a] for a in ("ia", "ja", "ka"))
    mesh = jax.sharding.Mesh(mesh.devices.reshape(ia, ja // 2, 2, ka), ("ia", "z", "c", "ka"))
    in_specs = (P("ia", ("z", "c"), "ka"), P(None, ("z", "c", "ka", "ia")), P(None, ("ka", "z", "c")))
    out_specs = (P(None, "ia", ("z", "c", "ka")), P(None, "ia"))
    return jax.shard_map(
        per_device, mesh=mesh, in_specs=in_specs, out_specs=out_specs, check_vma=False
    )
```

```python
import functools

import jax
import jax.numpy as jnp
from jax import lax
from jax.experimental import pallas as pl
from jax.experimental.pallas import tpu as pltpu
from jax.sharding import PartitionSpec as P

f32, bf16 = jnp.float32, jnp.bfloat16
R = 25
VM = pl.BlockSpec(memory_space=pltpu.VMEM)
HB = pl.BlockSpec(memory_space=pltpu.HBM)
TILES, BODY, MSG = 8, 200, 208
DIAGONALS = 13
BLOCK = 13


def lanes_of(shape):
    return lax.broadcasted_iota(jnp.int32, shape, 1)


def sublanes_of(shape):
    return lax.broadcasted_iota(jnp.int32, shape, 0)


def pad_rows(x, rows):
    return jnp.concatenate([x, jnp.zeros((rows - x.shape[0], x.shape[1]), x.dtype)], axis=0)


def fold(g):
    return jnp.concatenate([g[8 * q : 8 * q + 8] for q in range(4)], axis=1)


def unfold(g):
    return jnp.concatenate([g[:, 32 * q : 32 * q + 32] for q in range(4)], axis=0)


def transposed(x):
    rows = -(-x.shape[1] // 8) * 8
    x = jnp.concatenate([x, jnp.zeros((x.shape[0], 128 - x.shape[1]), x.dtype)], axis=1)
    return pad_rows(x, 128).T[0:rows, 0 : x.shape[0]]


def own_kernel(k_ref, j_ref, kout_ref, jout_ref, sems):
    copies = [pltpu.make_async_copy(k_ref, kout_ref, sems.at[0]), pltpu.make_async_copy(j_ref, jout_ref, sems.at[1])]
    for copy in copies:
        copy.start()
    for copy in copies:
        copy.wait()


def pack_kernel(k_ref, out_ref):
    k = pad_rows(k_ref[...].astype(f32), 32)
    folded = jnp.concatenate([k[0:16], k[16:32]], axis=1).astype(bf16)
    out_ref[...] = jnp.broadcast_to(folded[None], out_ref.shape)


def factor_kernel(j0, j1, j2, j3, out_ref):
    rows = jnp.concatenate([j[...].astype(f32) for j in (j0, j3, j2, j1)], axis=0)
    b = transposed(rows)
    out_ref[0:32, :] = pltpu.roll(jnp.concatenate([b, b], axis=1), lax.axis_index("ia") * 16, 1)
    rows = jnp.concatenate([rows, rows, jnp.zeros((64, 128 - 2 * R), f32)], axis=1)
    turned = [pltpu.roll(rows, 128 - d, 1) if d else rows for d in range(DIAGONALS)]
    diagonals = [jnp.sum(rows * x, axis=0, keepdims=True) for x in turned]
    diagonals = pad_rows(jnp.concatenate(diagonals, axis=0), 16)
    low = lanes_of((8, 128)) < 32
    out_ref[32:40, :] = jnp.where(low, diagonals[0:8], pltpu.roll(diagonals[8:16], 32, 1))


def part_copy(t_ref, dst, s, sem):
    dest = lax.rem(lax.axis_index("ka") + s, 4)
    block = t_ref.at[:, pl.ds(pl.multiple_of(dest * 64, 64), 64), :]
    return pltpu.make_async_copy(block, dst, sem)


ORDER = (2, 1, 3, 0)


def contract_kernel(c_ref, t_ref, *refs):
    msgs, held_ref, sems = refs[0:4], refs[4], refs[5]
    copies = [part_copy(t_ref, held_ref.at[s], s, sems.at[s]) for s in range(4)]
    for s in ORDER:
        copies[s].start()
    blocks = [c_ref[p].astype(f32) for p in range(16)]
    low = lanes_of((16, 128)) < 64
    tops, bottoms = [], []
    for a, b in zip(blocks[0::2], blocks[1::2]):
        tops.append(jnp.where(low, a, pltpu.roll(b, 64, 1)))
        bottoms.append(jnp.where(low, pltpu.roll(a, 64, 1), b))
    c = jnp.concatenate([jnp.concatenate(tops, axis=1), jnp.concatenate(bottoms, axis=1)], axis=0).astype(bf16)
    nt = (((1,), (1,)), ((), ()))
    gram = fold(lax.dot_general(c, c, nt, preferred_element_type=f32))
    for s in ORDER:
        copies[s].wait()
        y = lax.dot_general(c, held_ref[s].reshape(1024, 1024), nt, preferred_element_type=f32)
        for t in range(TILES):
            msgs[s][24 * t : 24 * t + 24, :] = y[0:24, 128 * t : 128 * t + 128]
            msgs[s][192 + t : 193 + t, :] = y[24:25, 128 * t : 128 * t + 128]
        msgs[s][BODY:MSG, :] = gram


def partial_kernel(y0, y1, y2, y3, b0, b1, b2, b3, pay_ref):
    ys, bs = (y0, y1, y2, y3), (b0, b1, b2, b3)
    lane24, low24 = lanes_of((24, 128)), lanes_of((24, 128)) < 64
    m = jnp.zeros((24, 128), f32)
    for t in range(TILES):
        at = slice(24 * t, 24 * t + 24)
        p = functools.reduce(jnp.add, [y[at, :] * b[0:24, :] for y, b in zip(ys, bs)])
        m = jnp.where(lane24 == 2 * t, jnp.sum(jnp.where(low24, p, 0.0), axis=1, keepdims=True), m)
        m = jnp.where(lane24 == 2 * t + 1, jnp.sum(jnp.where(low24, 0.0, p), axis=1, keepdims=True), m)
    p = functools.reduce(jnp.add, [y[192:200, :] * b[24:25, :] for y, b in zip(ys, bs)])
    low8 = lanes_of((8, 128)) < 64
    last = [jnp.sum(jnp.where(keep, p, 0.0), axis=1, keepdims=True) for keep in (low8, ~low8)]
    d = (b0[32:40, :] + b1[32:40, :]) + (b2[32:40, :] + b3[32:40, :])
    d = jnp.concatenate([d[:, 0:32], d[:, 32:64]], axis=0)
    d = pltpu.roll(d, lax.rem(16 - 4 * lax.axis_index("ka"), 16), 0)[0:4, 0:R]
    pay = [m[4 * q : 4 * q + 4, 0:16] for q in range(6)] + [d]
    pay += [x[v : v + 4] for v in (0, 4) for x in last] + [jnp.zeros((4, 3), f32)]
    pay_ref[...] = jnp.broadcast_to(jnp.concatenate(pay, axis=1)[None], pay_ref.shape)


def add_kernel(x_ref, out_ref):
    out_ref[...] = jnp.sum(x_ref[...].reshape(8, 4, 4, 128), axis=0)


def sum_kernel(y0, y1, y2, y3, y_ref, gk_ref):
    def total(at):
        return (y0[at, :] + y1[at, :]) + (y2[at, :] + y3[at, :])

    for t in range(TILES):
        s = total(slice(24 * t, 24 * t + 24))
        y_ref[pl.ds(2 * t, 24, stride=16), :] = s[:, 0:64]
        y_ref[pl.ds(2 * t + 1, 24, stride=16), :] = s[:, 64:128]
    s = total(slice(192, 200))
    y_ref[pl.ds(384, 8, stride=2), :] = s[:, 0:64]
    y_ref[pl.ds(385, 8, stride=2), :] = s[:, 64:128]
    gk_ref[...] = total(slice(BODY, MSG))


def solve_kernel(x0, x1, gk_ref, out_ref):
    gram_k = unfold(gk_ref[...])
    x = x0[...] + x1[...]
    d = jnp.concatenate([x[q][:, 96 : 96 + R] for q in range(4)], axis=0)
    x = (x[0] + x[1]) + (x[2] + x[3])
    lane, sub = lanes_of((4, 16)), sublanes_of((4, 16))
    last = jnp.zeros((4, 16), f32)
    for q in range(4):
        here = (lane // 8 == q // 2) & (lane % 2 == q % 2) & (lane // 2 % 4 == sub)
        last = jnp.where(here, x[:, 121 + q : 122 + q], last)
    last = jnp.sum(last, axis=0, keepdims=True)
    m = pad_rows(jnp.concatenate([x[:, 16 * q : 16 * q + 16] for q in range(6)] + [last], axis=0), 32)
    row, lane = sublanes_of((32, 32)), lanes_of((32, 32))
    d = jnp.concatenate([d, jnp.zeros((16, 32 - R), f32)], axis=1)
    apart = jnp.where(row < lane, row - lane + R, row - lane)
    gram = jnp.zeros((32, 32), f32)
    for q in range(1, DIAGONALS):
        gram = jnp.where(apart == q, d[q : q + 1, :], gram)
    gram = gram + transposed(gram)
    gram = jnp.where(apart == 0, d[0:1, :], gram)
    n = jnp.where((row < R) & (lane < R), gram * gram_k, 0.0)
    a = jnp.concatenate([n, m, jnp.zeros((32, 80), f32)], axis=1)
    row_at = sublanes_of((32, 128))
    for first in range(0, R, BLOCK):
        cols = [jnp.broadcast_to(a[:, p : p + 1], (32, 128)) for p in range(first, min(first + BLOCK, R))]
        for q in range(len(cols)):
            p = first + q
            scale = 1.0 / cols[q][p : p + 1, :]

            def eliminate(x):
                row = jnp.broadcast_to(x[p : p + 1, :] * scale, (32, 128))
                return jnp.where(row_at == p, row, x - cols[q] * row)

            a = eliminate(a)
            cols[q + 1 :] = [eliminate(x) for x in cols[q + 1 :]]
    out_ref[...] = pad_rows(a, 128).T[32:48, 0:R]


def call(kernel, out, specs, flops=0, nbytes=0, scratch=(), out_specs=None):
    return pl.pallas_call(
        kernel,
        out_shape=out,
        in_specs=specs,
        out_specs=out_specs or jax.tree.map(lambda _: VM, out),
        scratch_shapes=scratch,
        compiler_params=pltpu.CompilerParams(vmem_limit_bytes=12 * 2**20),
        cost_estimate=pl.CostEstimate(flops=flops, bytes_accessed=nbytes, transcendentals=0),
    )


def shift(x, axis, by, n):
    return lax.ppermute(x, axis, [(i, (i + by) % n) for i in range(n)])


def per_device(tensor, factor_j, factor_k):
    sds = jax.ShapeDtypeStruct
    dma = pltpu.SemaphoreType.DMA
    factor_k = pltpu.with_memory_space_constraint(factor_k, pltpu.HBM)
    tensor = pltpu.with_memory_space_constraint(tensor, pltpu.HBM)
    j0 = factor_j.T
    js = {s: shift(j0, "ia", s, 4) for s in (1, 3, 2)}
    k_own, j_own = call(
        own_kernel, [sds((R, 64), bf16), sds((16, R), bf16)], [HB, HB], 0, 0, [dma((2,))]
    )(factor_k, pltpu.with_memory_space_constraint(j0, pltpu.HBM))
    packed = call(pack_kernel, sds((16, 16, 128), bf16), [VM])(k_own)
    c = lax.all_to_all(packed, ("z", "c"), 0, 0, tiled=True)
    b = call(factor_kernel, sds((40, 128), f32), [VM] * 4, 2**33, 2**20)(j_own, js[1], js[2], js[3])
    bs = {s: shift(b, "ka", 4 - s, 4) for s in (1, 3, 2)}
    msgs = call(
        contract_kernel, [sds((MSG, 128), f32)] * 4, [VM, HB], 2**34, 2**23,
        [pltpu.VMEM((4, 16, 64, 1024), bf16), dma((4,))],
    )(c, tensor)
    got = {s: shift(msgs[s], "ka", s, 4) for s in (2, 1, 3)}
    pay = call(partial_kernel, sds((32, 4, 128), f32), [VM] * 8)(*msgs, b, bs[1], bs[2], bs[3])
    pay = lax.all_to_all(pay, ("z", "ka"), 0, 0, tiled=True)
    pay = call(add_kernel, sds((4, 4, 128), f32), [VM])(pay)
    other = lax.ppermute(pay, "c", [(0, 1), (1, 0)])
    y, gram_k = call(sum_kernel, [sds((400, 64), f32), sds((8, 128), f32)], [VM] * 4, 0, 2**21)(
        msgs[0], got[2], got[1], got[3]
    )
    new_factor = call(solve_kernel, sds((16, R), f32), [VM] * 3)(pay, other, gram_k)
    return y.reshape(R, 16, 64), new_factor.T


def solution(mesh):
    ia, ja, ka = (mesh.shape[a] for a in ("ia", "ja", "ka"))
    mesh = jax.sharding.Mesh(mesh.devices.reshape(ia, ja // 2, 2, ka), ("ia", "z", "c", "ka"))
    in_specs = (P("ia", ("z", "c"), "ka"), P(None, ("z", "c", "ka", "ia")), P(None, ("ka", "z", "c")))
    out_specs = (P(None, "ia", ("z", "c", "ka")), P(None, "ia"))
    return jax.shard_map(
        per_device, mesh=mesh, in_specs=in_specs, out_specs=out_specs, check_vma=False
    )
```

```python
import functools

import jax
import jax.numpy as jnp
from jax import lax
from jax.experimental import pallas as pl
from jax.experimental.pallas import tpu as pltpu
from jax.sharding import PartitionSpec as P

f32, bf16 = jnp.float32, jnp.bfloat16
R = 25
VM = pl.BlockSpec(memory_space=pltpu.VMEM)
HB = pl.BlockSpec(memory_space=pltpu.HBM)
TILES, BODY, MSG = 8, 200, 208
DIAGONALS = 13
BLOCK = 13


def lanes_of(shape):
    return lax.broadcasted_iota(jnp.int32, shape, 1)


def sublanes_of(shape):
    return lax.broadcasted_iota(jnp.int32, shape, 0)


def pad_rows(x, rows):
    return jnp.concatenate([x, jnp.zeros((rows - x.shape[0], x.shape[1]), x.dtype)], axis=0)


def fold(g):
    return jnp.concatenate([g[8 * q : 8 * q + 8] for q in range(4)], axis=1)


def unfold(g):
    return jnp.concatenate([g[:, 32 * q : 32 * q + 32] for q in range(4)], axis=0)


def transposed(x):
    rows = -(-x.shape[1] // 8) * 8
    x = jnp.concatenate([x, jnp.zeros((x.shape[0], 128 - x.shape[1]), x.dtype)], axis=1)
    return x.T[0:rows]


def own_kernel(k_ref, j_ref, kout_ref, jout_ref, sems):
    copies = [pltpu.make_async_copy(k_ref, kout_ref, sems.at[0]), pltpu.make_async_copy(j_ref, jout_ref, sems.at[1])]
    for copy in copies:
        copy.start()
    for copy in copies:
        copy.wait()


def pack_kernel(k_ref, out_ref):
    k = pad_rows(k_ref[...].astype(f32), 32)
    folded = jnp.concatenate([k[0:16], k[16:32]], axis=1).astype(bf16)
    out_ref[...] = jnp.broadcast_to(folded[None], out_ref.shape)


def factor_kernel(j0, j1, j2, j3, out_ref):
    rows = jnp.concatenate([j[...].astype(f32) for j in (j0, j3, j2, j1)], axis=0)
    b = transposed(rows)
    out_ref[0:32, :] = pltpu.roll(jnp.concatenate([b, b], axis=1), lax.axis_index("ia") * 16, 1)
    rows = jnp.concatenate([rows, rows, jnp.zeros((64, 128 - 2 * R), f32)], axis=1)
    turned = [pltpu.roll(rows, 128 - d, 1) if d else rows for d in range(DIAGONALS)]
    diagonals = [jnp.sum(rows * x, axis=0, keepdims=True) for x in turned]
    diagonals = pad_rows(jnp.concatenate(diagonals, axis=0), 16)
    low = lanes_of((8, 128)) < 32
    out_ref[32:40, :] = jnp.where(low, diagonals[0:8], pltpu.roll(diagonals[8:16], 32, 1))


def part_copy(t_ref, dst, s, sem):
    dest = lax.rem(lax.axis_index("ka") + s, 4)
    block = t_ref.at[:, pl.ds(pl.multiple_of(dest * 64, 64), 64), :]
    return pltpu.make_async_copy(block, dst, sem)


ORDER = (2, 1, 3, 0)


def contract_kernel(c_ref, t_ref, *refs):
    msgs, held_ref, sems = refs[0:4], refs[4], refs[5]
    copies = [part_copy(t_ref, held_ref.at[s], s, sems.at[s]) for s in range(4)]
    for s in ORDER:
        copies[s].start()
    blocks = [c_ref[p].astype(f32) for p in range(16)]
    low = lanes_of((16, 128)) < 64
    tops, bottoms = [], []
    for a, b in zip(blocks[0::2], blocks[1::2]):
        tops.append(jnp.where(low, a, pltpu.roll(b, 64, 1)))
        bottoms.append(jnp.where(low, pltpu.roll(a, 64, 1), b))
    c = jnp.concatenate([jnp.concatenate(tops, axis=1), jnp.concatenate(bottoms, axis=1)], axis=0).astype(bf16)
    nt = (((1,), (1,)), ((), ()))
    gram = fold(lax.dot_general(c, c, nt, preferred_element_type=f32))
    for s in ORDER:
        copies[s].wait()
        y = lax.dot_general(c, held_ref[s].reshape(1024, 1024), nt, preferred_element_type=f32)
        for t in range(TILES):
            msgs[s][24 * t : 24 * t + 24, :] = y[0:24, 128 * t : 128 * t + 128]
            msgs[s][192 + t : 193 + t, :] = y[24:25, 128 * t : 128 * t + 128]
        msgs[s][BODY:MSG, :] = gram


def partial_kernel(y0, y1, y2, y3, b0, b1, b2, b3, pay_ref):
    ys, bs = (y0, y1, y2, y3), (b0, b1, b2, b3)
    lane24, low24 = lanes_of((24, 128)), lanes_of((24, 128)) < 64
    m = jnp.zeros((24, 128), f32)
    for t in range(TILES):
        at = slice(24 * t, 24 * t + 24)
        p = functools.reduce(jnp.add, [y[at, :] * b[0:24, :] for y, b in zip(ys, bs)])
        m = jnp.where(lane24 == 2 * t, jnp.sum(jnp.where(low24, p, 0.0), axis=1, keepdims=True), m)
        m = jnp.where(lane24 == 2 * t + 1, jnp.sum(jnp.where(low24, 0.0, p), axis=1, keepdims=True), m)
    p = functools.reduce(jnp.add, [y[192:200, :] * b[24:25, :] for y, b in zip(ys, bs)])
    low8 = lanes_of((8, 128)) < 64
    last = [jnp.sum(jnp.where(keep, p, 0.0), axis=1, keepdims=True) for keep in (low8, ~low8)]
    d = (b0[32:40, :] + b1[32:40, :]) + (b2[32:40, :] + b3[32:40, :])
    d = jnp.concatenate([d[:, 0:32], d[:, 32:64]], axis=0)
    d = pltpu.roll(d, lax.rem(16 - 4 * lax.axis_index("ka"), 16), 0)[0:4, 0:R]
    pay = [m[4 * q : 4 * q + 4, 0:16] for q in range(6)] + [d]
    pay += [x[v : v + 4] for v in (0, 4) for x in last] + [jnp.zeros((4, 3), f32)]
    pay_ref[...] = jnp.broadcast_to(jnp.concatenate(pay, axis=1)[None], pay_ref.shape)


def add_kernel(x_ref, out_ref):
    out_ref[...] = jnp.sum(x_ref[...].reshape(8, 4, 4, 128), axis=0)


def sum_kernel(y0, y1, y2, y3, y_ref, gk_ref):
    def total(at):
        return (y0[at, :] + y1[at, :]) + (y2[at, :] + y3[at, :])

    for t in range(TILES):
        s = total(slice(24 * t, 24 * t + 24))
        y_ref[pl.ds(2 * t, 24, stride=16), :] = s[:, 0:64]
        y_ref[pl.ds(2 * t + 1, 24, stride=16), :] = s[:, 64:128]
    s = total(slice(192, 200))
    y_ref[pl.ds(384, 8, stride=2), :] = s[:, 0:64]
    y_ref[pl.ds(385, 8, stride=2), :] = s[:, 64:128]
    gk_ref[...] = total(slice(BODY, MSG))


def solve_kernel(x0, x1, gk_ref, out_ref):
    gram_k = unfold(gk_ref[...])
    x = x0[...] + x1[...]
    d = jnp.concatenate([x[q][:, 96 : 96 + R] for q in range(4)], axis=0)
    x = (x[0] + x[1]) + (x[2] + x[3])
    lane, sub = lanes_of((4, 16)), sublanes_of((4, 16))
    last = jnp.zeros((4, 16), f32)
    for q in range(4):
        here = (lane // 8 == q // 2) & (lane % 2 == q % 2) & (lane // 2 % 4 == sub)
        last = jnp.where(here, x[:, 121 + q : 122 + q], last)
    last = jnp.sum(last, axis=0, keepdims=True)
    m = pad_rows(jnp.concatenate([x[:, 16 * q : 16 * q + 16] for q in range(6)] + [last], axis=0), 32)
    row, lane = sublanes_of((32, 32)), lanes_of((32, 32))
    d = jnp.concatenate([d, jnp.zeros((16, 32 - R), f32)], axis=1)
    apart = jnp.where(row < lane, row - lane + R, row - lane)
    gram = jnp.zeros((32, 32), f32)
    for q in range(1, DIAGONALS):
        gram = jnp.where(apart == q, d[q : q + 1, :], gram)
    gram = gram + transposed(gram)
    gram = jnp.where(apart == 0, d[0:1, :], gram)
    n = jnp.where((row < R) & (lane < R), gram * gram_k, 0.0)
    a = jnp.concatenate([n, m, jnp.zeros((32, 80), f32)], axis=1)
    row_at = sublanes_of((32, 128))
    for first in range(0, R, BLOCK):
        cols = [jnp.broadcast_to(a[:, p : p + 1], (32, 128)) for p in range(first, min(first + BLOCK, R))]
        for q in range(len(cols)):
            p = first + q
            scale = 1.0 / cols[q][p : p + 1, :]

            def eliminate(x):
                row = jnp.broadcast_to(x[p : p + 1, :] * scale, (32, 128))
                return jnp.where(row_at == p, row, x - cols[q] * row)

            a = eliminate(a)
            cols[q + 1 :] = [eliminate(x) for x in cols[q + 1 :]]
    out_ref[...] = a.T[32:48, 0:R]


def call(kernel, out, specs, flops=0, nbytes=0, scratch=(), out_specs=None):
    return pl.pallas_call(
        kernel,
        out_shape=out,
        in_specs=specs,
        out_specs=out_specs or jax.tree.map(lambda _: VM, out),
        scratch_shapes=scratch,
        compiler_params=pltpu.CompilerParams(vmem_limit_bytes=12 * 2**20),
        cost_estimate=pl.CostEstimate(flops=flops, bytes_accessed=nbytes, transcendentals=0),
    )


def shift(x, axis, by, n):
    return lax.ppermute(x, axis, [(i, (i + by) % n) for i in range(n)])


def per_device(tensor, factor_j, factor_k):
    sds = jax.ShapeDtypeStruct
    dma = pltpu.SemaphoreType.DMA
    factor_k = pltpu.with_memory_space_constraint(factor_k, pltpu.HBM)
    tensor = pltpu.with_memory_space_constraint(tensor, pltpu.HBM)
    j0 = factor_j.T
    js = {s: shift(j0, "ia", s, 4) for s in (1, 3, 2)}
    k_own, j_own = call(
        own_kernel, [sds((R, 64), bf16), sds((16, R), bf16)], [HB, HB], 0, 0, [dma((2,))]
    )(factor_k, pltpu.with_memory_space_constraint(j0, pltpu.HBM))
    packed = call(pack_kernel, sds((16, 16, 128), bf16), [VM])(k_own)
    c = lax.all_to_all(packed, ("z", "c"), 0, 0, tiled=True)
    b = call(factor_kernel, sds((40, 128), f32), [VM] * 4, 2**33, 2**20)(j_own, js[1], js[2], js[3])
    bs = {s: shift(b, "ka", 4 - s, 4) for s in (1, 3, 2)}
    msgs = call(
        contract_kernel, [sds((MSG, 128), f32)] * 4, [VM, HB], 2**34, 2**23,
        [pltpu.VMEM((4, 16, 64, 1024), bf16), dma((4,))],
    )(c, tensor)
    got = {s: shift(msgs[s], "ka", s, 4) for s in (2, 1, 3)}
    pay = call(partial_kernel, sds((32, 4, 128), f32), [VM] * 8)(*msgs, b, bs[1], bs[2], bs[3])
    pay = lax.all_to_all(pay, ("z", "ka"), 0, 0, tiled=True)
    pay = call(add_kernel, sds((4, 4, 128), f32), [VM])(pay)
    other = lax.ppermute(pay, "c", [(0, 1), (1, 0)])
    y, gram_k = call(sum_kernel, [sds((400, 64), f32), sds((8, 128), f32)], [VM] * 4, 0, 2**21)(
        msgs[0], got[2], got[1], got[3]
    )
    new_factor = call(solve_kernel, sds((16, R), f32), [VM] * 3)(pay, other, gram_k)
    return y.reshape(R, 16, 64), new_factor.T


def solution(mesh):
    ia, ja, ka = (mesh.shape[a] for a in ("ia", "ja", "ka"))
    mesh = jax.sharding.Mesh(mesh.devices.reshape(ia, ja // 2, 2, ka), ("ia", "z", "c", "ka"))
    in_specs = (P("ia", ("z", "c"), "ka"), P(None, ("z", "c", "ka", "ia")), P(None, ("ka", "z", "c")))
    out_specs = (P(None, "ia", ("z", "c", "ka")), P(None, "ia"))
    return jax.shard_map(
        per_device, mesh=mesh, in_specs=in_specs, out_specs=out_specs, check_vma=False
    )
```
